32 devices in a mesh: seq: 16 (over z, x, core), ch: 2 (over y).
Axes of the slice: x: 2, y: 2, z: 4, core: 2. Of those that a mesh axis runs over, the one named last changes fastest.
Arguments:
- q_proj: bfloat16 [4096, 8192], P('seq', 'ch'), may hold values from -60 to 60
- k_proj: bfloat16 [4096, 8192], P('seq', 'ch'), may hold values from -6 to 6
- v_proj: bfloat16 [4096, 8192], P('seq', 'ch'), may hold values from -6 to 6
- short_filter: float32 [9, 8192], P(None, 'ch'), may hold values from -3 to 3
- log_decay: float32 [512, 16], P('ch'), may hold values from -0.1 to -0.00012207031
- residue: float32 [512, 16], P('ch'), may hold values from -15 to 15
- skip_bias: float32 [8192], P('ch'), may hold values from -4 to 4
- norm_gain: float32 [8192], P('ch'), may hold values from 0.25 to 1.75
Outputs:
- mixed_out: bfloat16 [4096, 8192], P('seq', 'ch')
The draws below stay inside these ranges and needn't reach their ends.
All inputs are finite; a program needn't handle non-finite values.
Results may differ from the reference program's by a relative error of at most 0.0058.
Values may be sent and summed in bfloat16 or wider, within the bound.
A program may use at most 128 MiB of HBM per device.

```python
import math
import jax
import jax.numpy as jnp
from jax import lax

D = 8192
GROUP = 16
MODES = 16
TOK_DEV = 256
LENGTH = 4096
GROUPS = 512


def draw_q_proj(key, part):
    key_one, key_two = jax.random.split(key)
    values = jnp.clip(jax.random.normal(key_one, (LENGTH, D), jnp.float32), -6.0, 6.0)
    row_scale = jnp.exp(math.log(10.0) * jax.random.uniform(key_two, (LENGTH, 1), jnp.float32))
    return (values * row_scale).astype(jnp.bfloat16)


def draw_log_decay(key, part):
    key_one, key_two, key_three, key_four = jax.random.split(key, 4)
    slow_rate = jnp.exp(jax.random.uniform(key_one, (GROUPS, MODES), jnp.float32, math.log(0.5), math.log(2.0))) / LENGTH
    middle_rate = jnp.exp(jax.random.uniform(key_two, (GROUPS, MODES), jnp.float32, math.log(0.3), math.log(4.0))) / TOK_DEV
    middle_rate = jnp.minimum(middle_rate, 0.1)
    fast_rate = jnp.exp(jax.random.uniform(key_three, (GROUPS, MODES), jnp.float32, math.log(0.02), math.log(0.1)))
    share_slow = 0.4
    share_middle = 0.35
    picker = jax.random.uniform(key_four, (GROUPS, MODES), jnp.float32)
    is_slow = picker < share_slow
    is_middle = jnp.logical_and(picker >= share_slow, picker < share_slow + share_middle)
    rate = jnp.where(is_slow, slow_rate, jnp.where(is_middle, middle_rate, fast_rate))
    return -rate


def draw_residue(key, part):
    values = jnp.clip(jax.random.normal(key, (GROUPS, MODES), jnp.float32), -6.0, 6.0)
    group_scale = 0.25 * jnp.exp(math.log(10.0) * jnp.arange(GROUPS, dtype=jnp.float32) / GROUPS)
    return values * group_scale[:, None]


def levels(rng, extent, pieces, least, high):
    level = 1.0
    for position, blocks in pieces:
        steps = jax.random.uniform(jax.random.fold_in(jax.random.fold_in(rng, 6), position), (blocks,), jnp.float32, least / len(pieces), high / len(pieces))
        level = level * jnp.repeat(jnp.exp(steps), extent[position] // blocks).reshape((-1,) + (1,) * (len(extent) - 1 - position))
    return level


def gaussian(stream_key, extent, scale, most, shards=(), kind=jnp.bfloat16):
    values = jax.random.normal(stream_key, extent, jnp.float32) * scale
    if len(shards) > 0:
        values = levels(stream_key, extent, shards, -0.22, 0.18) * values
    return jnp.clip(values, min=-most, max=most).astype(kind)


def setup_inputs(seed: int = 0) -> dict:
    key_list = jax.random.split(jax.random.key(seed), 9)
    q_proj = draw_q_proj(jax.random.fold_in(key_list[8], 71), 0)
    k_proj = gaussian(key_list[1], (LENGTH, D), 1.0, 6.0, ((0, 16), (1, 2)))
    v_proj = gaussian(key_list[2], (LENGTH, D), 1.0, 6.0, ((0, 16), (1, 2)))
    short_filter = gaussian(key_list[3], (9, D), 0.5, 3.0, ((1, 2),), jnp.float32)
    log_decay = draw_log_decay(jax.random.fold_in(key_list[8], 71), 0)
    residue = draw_residue(jax.random.fold_in(key_list[8], 71), 0)
    skip_bias = gaussian(key_list[6], (D,), 1.0, 4.0, ((0, 2),), jnp.float32)
    norm_gain = jnp.clip(1.0 + 0.15 * jax.random.normal(key_list[7], (D,), jnp.float32), 0.25, 1.75)
    return dict(q_proj=q_proj, k_proj=k_proj, v_proj=v_proj, short_filter=short_filter, log_decay=log_decay, residue=residue, skip_bias=skip_bias, norm_gain=norm_gain)


def short_conv(current, earlier, taps):
    padded = jnp.concatenate([earlier, current], axis=0)
    return taps[0] * padded[2:] + taps[1] * padded[1:-1] + taps[2] * padded[:-2]

def block_toeplitz(log_decay, weight, block):
    groups, modes = log_decay.shape
    offsets = (jnp.arange(block)[:, None] - jnp.arange(block)[None, :]).astype(jnp.float32)
    causal = offsets >= 0.0
    lagged = jnp.maximum(offsets, 0.0)
    toeplitz = jnp.zeros((groups, block, block), jnp.float32)
    for mode_index in range(modes):
        rate = log_decay[:, mode_index][:, None, None]
        toeplitz = toeplitz + weight[:, mode_index][:, None, None] * jnp.exp(lagged[None] * rate)
    return jnp.where(causal[None], toeplitz, jnp.float32(0.0))

def local_filter(mixed_in, log_decay, weight, size_group):
    tok_rows, channels = mixed_in.shape
    groups, modes = log_decay.shape
    block = min(128, tok_rows)
    count = tok_rows // block
    highest = lax.Precision.HIGHEST
    lag = jnp.arange(block, dtype=jnp.float32)
    toeplitz = block_toeplitz(log_decay, weight, block)
    entering = jnp.exp((lag + 1.0)[None, :, None] * log_decay[:, None, :]) * weight[:, None, :]
    leaving = jnp.exp((block - 1.0 - lag)[None, :, None] * log_decay[:, None, :])
    block_decay = jnp.exp(block * log_decay)
    blocks = mixed_in.reshape(count, block, groups, size_group)

    def advance(state, inputs_block):
        values = inputs_block.astype(jnp.float32)
        local_part = jnp.einsum('gab,bgk->agk', toeplitz, values, precision=highest)
        carried = jnp.einsum('gam,gkm->agk', entering, state, precision=highest)
        new_state = state * block_decay[:, None, :] + jnp.einsum('gbm,bgk->gkm', leaving, values, precision=highest)
        return (new_state, local_part + carried)
    start_state = jnp.zeros((groups, size_group, modes), jnp.float32)
    final_state, outputs = lax.scan(advance, start_state, blocks)
    return (outputs.reshape(tok_rows, channels), final_state)

def reference(q_proj, k_proj, v_proj, short_filter, log_decay, residue, skip_bias, norm_gain):
    zero_rows = jnp.zeros((2, D), jnp.float32)
    q_short = short_conv(q_proj.astype(jnp.float32), zero_rows, short_filter[0:3]).astype(jnp.bfloat16)
    q_short = lax.optimization_barrier(q_short)
    k_short = short_conv(k_proj.astype(jnp.float32), zero_rows, short_filter[3:6])
    v_short = short_conv(v_proj.astype(jnp.float32), zero_rows, short_filter[6:9])
    mixed_in = (k_short * v_short).astype(jnp.bfloat16)
    mixed_in = lax.optimization_barrier(mixed_in)
    pole = jnp.exp(log_decay)
    weight = residue * jnp.sqrt(1.0 - pole * pole)
    conv_out, final_state = local_filter(mixed_in, log_decay, weight, GROUP)
    filtered = conv_out + skip_bias * mixed_in.astype(jnp.float32)
    gated = q_short.astype(jnp.float32) * filtered
    mean_square = lax.optimization_barrier(jnp.mean(gated * gated, axis=1, keepdims=True))
    return (gated * lax.rsqrt(mean_square + 1e-05) * norm_gain).astype(jnp.bfloat16)
```

```python
import functools
import jax
import jax.numpy as jnp
from jax import lax
from jax.experimental import pallas as pl
from jax.experimental.pallas import tpu as pltpu
from jax.sharding import PartitionSpec as P

LANES = 128
MESH = pl.DeviceIdType.MESH
f32 = jnp.float32
bf16 = jnp.bfloat16


def tile_at(i):
    return pl.ds(pl.multiple_of(i * LANES, LANES), LANES)


def kernel(n, nch, rounds, modes, q_ref, k_ref, v_ref, taps_ref, decay_ref, residue_ref, skip_ref, gain_ref,
           out_ref, halo_out, halo_in, pad, leaving, hrev, entering, mixed, conv, rate, wide_weight,
           total, carry, state_out, state_in, square, square_out, square_in,
           halo_send, halo_recv, state_send, state_recv, square_send, square_recv):
    tok, channels = q_ref.shape
    half = tok // 2
    tiles = channels // LANES
    per = LANES // modes
    me = lax.axis_index("seq")
    mych = lax.axis_index("ch")
    right, left = lax.rem(me + 1, n), lax.rem(me + n - 1, n)

    def partner(bit):
        return me + bit * (1 - 2 * lax.rem(lax.div(me, bit), 2))

    barrier = pltpu.get_barrier_semaphore()
    for other in [right, left] + [partner(1 << r) for r in range(rounds)]:
        pl.semaphore_signal(barrier, inc=1, device_id={"seq": other}, device_id_type=MESH)
    for d in range(1, nch):
        pl.semaphore_signal(barrier, inc=1, device_id={"ch": lax.rem(mych + d, nch)}, device_id_type=MESH)

    halo_out[...] = jnp.zeros_like(halo_out)
    for j, ref in enumerate((q_ref, k_ref, v_ref)):
        halo_out[2 * j:2 * j + 2, :] = ref[tok - 16:tok, :].astype(f32)[14:16]
    pl.semaphore_wait(barrier, 2 + rounds + nch - 1)

    halo = pltpu.make_async_remote_copy(halo_out, halo_in, halo_send, halo_recv,
                                        device_id={"seq": right}, device_id_type=MESH)

    @pl.when(me < n - 1)
    def _():
        halo.start()

    lane = lax.broadcasted_iota(jnp.int32, (1, LANES), 1)
    lane_group = lane // modes
    lags_rev = (tok - 1 - lax.broadcasted_iota(jnp.int32, (1, tok), 1)).astype(f32)

    spread = (lax.broadcasted_iota(jnp.int32, (modes, LANES), 1) % modes
              == lax.broadcasted_iota(jnp.int32, (modes, LANES), 0)).astype(f32)
    after = (lax.broadcasted_iota(jnp.int32, (tok, 1), 0) + 1).astype(f32)
    sub = lax.broadcasted_iota(jnp.int32, (per, LANES), 0)
    sub_lane = lax.broadcasted_iota(jnp.int32, (per, LANES), 1) // modes

    def prepare(i, _):
        logs = decay_ref[pl.ds(pl.multiple_of(i * per, per), per), :]
        res = residue_ref[pl.ds(pl.multiple_of(i * per, per), per), :]
        pole = jnp.exp(logs)
        weight = res * jnp.sqrt(1.0 - pole * pole)
        cols, wcols = logs.T, weight.T
        rows = []
        wide_rate = jnp.zeros((modes, LANES), f32)
        wide_w = jnp.zeros((modes, LANES), f32)
        for j in range(per):
            col, wcol = cols[:, j:j + 1], wcols[:, j:j + 1]
            power = jnp.exp(col * lags_rev)
            leaving[pl.ds(pl.multiple_of(i * LANES, LANES) + j * modes, modes), :] = power.astype(bf16)
            rows.append(jnp.sum(power * wcol, axis=0, keepdims=True))
            wide_rate = jnp.where(lane_group == j, col, wide_rate)
            wide_w = jnp.where(lane_group == j, wcol, wide_w)
        hrev[pl.ds(pl.multiple_of(i * per, per), per), :] = jnp.concatenate(rows, axis=0)
        rate[:, tile_at(i)] = wide_rate
        wide_weight[:, tile_at(i)] = wide_w
        return 0

    lax.fori_loop(0, tiles, prepare, 0)

    @pl.when(me > 0)
    def _():
        halo.wait_recv()

    @pl.when(me == 0)
    def _():
        halo_in[...] = jnp.zeros_like(halo_in)

    def short(ref, which, i):
        pad[which, 8:8 + tok, :] = ref[:, tile_at(i)].astype(f32)
        pad[which, 0:8, :] = jnp.concatenate(
            [jnp.zeros((6, LANES), f32), halo_in[2 * which:2 * which + 2, tile_at(i)]], axis=0)
        a = [taps_ref[3 * which + t:3 * which + t + 1, tile_at(i)] for t in range(3)]
        return a[0] * pad[which, 8:8 + tok, :] + a[1] * pad[which, 7:7 + tok, :] + a[2] * pad[which, 6:6 + tok, :]

    def summarize(i, _):
        values = (short(k_ref, 1, i) * short(v_ref, 2, i)).astype(bf16)
        mixed[:, tile_at(i)] = values
        spreadout = jnp.dot(leaving[tile_at(i), :], values, preferred_element_type=f32)
        state = jnp.zeros((modes, LANES), f32)
        for j in range(per):
            state = jnp.where(lane_group == j, spreadout[j * modes:(j + 1) * modes], state)
        total[:, tile_at(i)] = state
        state_out[0, :, tile_at(i)] = state.astype(bf16)
        carry[:, tile_at(i)] = jnp.zeros((modes, LANES), f32)
        return 0

    lax.fori_loop(0, tiles, summarize, 0)

    causal = (lax.broadcasted_iota(jnp.int32, (half, tok), 1)
              <= lax.broadcasted_iota(jnp.int32, (half, tok), 0) + half)

    def convolve(i, _):
        values = mixed[:, tile_at(i)]
        first, second = values[:half], values[half:]
        right_side = jnp.concatenate(
            [jnp.concatenate([jnp.zeros_like(first), first], axis=1),
             jnp.concatenate([first, second], axis=1)], axis=0)
        lines = hrev[pl.ds(pl.multiple_of(i * per, per), per), :]
        blocks = []
        for j in range(per):
            line = jnp.broadcast_to(lines[j:j + 1], (half, tok))
            block = pltpu.roll(line, half + 1, 1, stride=1, stride_axis=0)
            blocks.append(jnp.where(causal, block, 0.0).astype(bf16))
        product = jnp.dot(jnp.concatenate(blocks, axis=0), right_side, preferred_element_type=f32)
        low = jnp.zeros((half, LANES), f32)
        high = jnp.zeros((half, LANES), f32)
        for j in range(per):
            part = product[j * half:(j + 1) * half]
            low = jnp.where(lane_group == j, part[:, :LANES], low)
            high = jnp.where(lane_group == j, part[:, LANES:], high)
        skip = skip_ref[:, tile_at(i)]
        conv[:half, tile_at(i)] = low + skip * first.astype(f32)
        conv[half:, tile_at(i)] = high + skip * second.astype(f32)
        logs = decay_ref[pl.ds(pl.multiple_of(i * per, per), per), :]
        row = jnp.dot(logs, spread, preferred_element_type=f32, precision=lax.Precision.HIGHEST)
        row = jnp.sum(jnp.where(sub == sub_lane, row, 0.0), axis=0, keepdims=True)
        entering[:, tile_at(i)] = jnp.exp(after * row).astype(bf16)
        return 0

    for r in range(rounds):
        bit = 1 << r
        last = r == rounds - 1
        upper = lax.rem(lax.div(me, bit), 2) == 1
        copy = pltpu.make_async_remote_copy(state_out.at[r], state_in.at[r], state_send.at[r], state_recv.at[r],
                                            device_id={"seq": partner(bit)}, device_id_type=MESH)
        if last:
            @pl.when(jnp.logical_not(upper))
            def _():
                copy.start()
        else:
            copy.start()
        lax.fori_loop(tiles * r // rounds, tiles * (r + 1) // rounds, convolve, 0)
        block_rate = float(tok * bit)
        offset = (lax.rem(me, bit) * tok).astype(f32)

        def merge(i, _):
            theirs = state_in[r, :, tile_at(i)].astype(f32)
            logs = rate[:, tile_at(i)]
            inward = jnp.exp(logs * offset) * theirs
            carry[:, tile_at(i)] += jnp.where(upper, inward, 0.0)
            if not last:
                mine = total[:, tile_at(i)]
                later = jnp.where(upper, mine, theirs)
                before = jnp.where(upper, theirs, mine)
                both = jnp.exp(logs * block_rate) * before + later
                total[:, tile_at(i)] = both
                state_out[r + 1, :, tile_at(i)] = both.astype(bf16)
            return 0

        if last:
            @pl.when(upper)
            def _():
                copy.wait_recv()
                lax.fori_loop(0, tiles, merge, 0)
        else:
            copy.wait_recv()
            lax.fori_loop(0, tiles, merge, 0)

    square[...] = jnp.zeros_like(square)

    def gate(i, _):
        state = carry[:, tile_at(i)] * wide_weight[:, tile_at(i)]
        diagonal = jnp.concatenate([jnp.where(lane_group == j, state, 0.0) for j in range(per)], axis=0)
        fine = diagonal.astype(bf16)
        rest = (diagonal - fine.astype(f32)).astype(bf16)
        ent = entering[:, tile_at(i)]
        carried = jnp.dot(jnp.concatenate([ent, ent], axis=1), jnp.concatenate([fine, rest], axis=0),
                          preferred_element_type=f32)
        q_short = short(q_ref, 0, i).astype(bf16).astype(f32)
        gated = q_short * (conv[:, tile_at(i)] + carried)
        conv[:, tile_at(i)] = gated
        square[...] += gated * gated
        return 0

    lax.fori_loop(0, tiles, gate, 0)

    sums = jnp.sum(square[...].T, axis=0, keepdims=True)
    square_out[...] = jnp.broadcast_to(sums, square_out.shape)
    copies = []
    for d in range(1, nch):
        c = pltpu.make_async_remote_copy(square_out, square_in.at[d - 1], square_send.at[d - 1], square_recv.at[d - 1],
                                         device_id={"ch": lax.rem(mych + d, nch)}, device_id_type=MESH)
        c.start()
        copies.append(c)
    for d, c in enumerate(copies):
        c.wait()
        sums = sums + square_in[d, 0:1, :]
    scale = lax.rsqrt(sums / (channels * nch) + 1e-5)
    square[...] = jnp.broadcast_to(scale, (LANES, tok)).T

    def finish(i, _):
        out_ref[:, tile_at(i)] = (conv[:, tile_at(i)] * square[...] * gain_ref[:, tile_at(i)]).astype(bf16)
        return 0

    lax.fori_loop(0, tiles, finish, 0)

    @pl.when(me < n - 1)
    def _():
        halo.wait_send()

    for r in range(rounds):
        bit = 1 << r
        copy = pltpu.make_async_remote_copy(state_out.at[r], state_in.at[r], state_send.at[r], state_recv.at[r],
                                            device_id={"seq": partner(bit)}, device_id_type=MESH)
        if r == rounds - 1:
            @pl.when(lax.rem(lax.div(me, bit), 2) == 0)
            def _():
                copy.wait_send()
        else:
            copy.wait_send()


def on_device(n, nch, q_proj, k_proj, v_proj, short_filter, log_decay, residue, skip_bias, norm_gain):
    tok, channels = q_proj.shape
    groups, modes = log_decay.shape
    rounds = n.bit_length() - 1
    assert n == 1 << rounds and channels == groups * modes
    vmem = pl.BlockSpec(memory_space=pltpu.VMEM)
    dma = pltpu.SemaphoreType.DMA
    return pl.pallas_call(
        functools.partial(kernel, n, nch, rounds, modes),
        out_shape=jax.ShapeDtypeStruct((tok, channels), bf16),
        in_specs=[vmem] * 8,
        out_specs=vmem,
        scratch_shapes=[
            pltpu.VMEM((8, channels), f32),
            pltpu.VMEM((8, channels), f32),
            pltpu.VMEM((3, tok + 8, LANES), f32),
            pltpu.VMEM((channels, tok), bf16),
            pltpu.VMEM((groups, tok), f32),
            pltpu.VMEM((tok, channels), bf16),
            pltpu.VMEM((tok, channels), bf16),
            pltpu.VMEM((tok, channels), f32),
            pltpu.VMEM((modes, channels), f32),
            pltpu.VMEM((modes, channels), f32),
            pltpu.VMEM((modes, channels), f32),
            pltpu.VMEM((modes, channels), f32),
            pltpu.VMEM((rounds, modes, channels), bf16),
            pltpu.VMEM((rounds, modes, channels), bf16),
            pltpu.VMEM((tok, LANES), f32),
            pltpu.VMEM((8, tok), f32),
            pltpu.VMEM((max(nch - 1, 1), 8, tok), f32),
            dma, dma, dma((rounds,)), dma((rounds,)), dma((max(nch - 1, 1),)), dma((max(nch - 1, 1),)),
        ],
        compiler_params=pltpu.CompilerParams(collective_id=0, has_side_effects=True,
                                             vmem_limit_bytes=50 * 1024 * 1024),
    )(q_proj, k_proj, v_proj, short_filter, log_decay, residue,
      skip_bias.reshape(1, channels), norm_gain.reshape(1, channels))


def solution(mesh):
    return jax.shard_map(
        functools.partial(on_device, mesh.shape["seq"], mesh.shape["ch"]),
        mesh=mesh,
        in_specs=(P("seq", "ch"), P("seq", "ch"), P("seq", "ch"), P(None, "ch"),
                  P("ch", None), P("ch", None), P("ch"), P("ch")),
        out_specs=P("seq", "ch"),
        check_vma=False,
    )
```

```python
import functools
import jax
import jax.numpy as jnp
from jax import lax
from jax.experimental import pallas as pl
from jax.experimental.pallas import tpu as pltpu
from jax.sharding import PartitionSpec as P

LANES = 128
MESH = pl.DeviceIdType.MESH
f32 = jnp.float32
bf16 = jnp.bfloat16


def tile_at(i):
    return pl.ds(pl.multiple_of(i * LANES, LANES), LANES)


def kernel(n, nch, rounds, modes, q_hbm, k_hbm, v_hbm, taps_hbm, decay_hbm, residue_hbm, skip_hbm, gain_hbm,
           out_ref, q_ref, k_ref, v_ref, taps_ref, decay_flat, residue_flat, skip_ref, gain_ref,
           tails, decay_ref, residue_ref, halo_out, halo_in, pad, leaving, hrev, entering, mixed, conv, rate, wide_weight,
           total, carry, state_out, state_in, square, square_out, square_in,
           halo_send, halo_recv, state_send, state_recv, square_send, square_recv, load_sem, tail_sem):
    tok, channels = q_ref.shape
    half = tok // 2
    tiles = channels // LANES
    per = LANES // modes
    me = lax.axis_index("seq")
    mych = lax.axis_index("ch")
    right, left = lax.rem(me + 1, n), lax.rem(me + n - 1, n)

    def partner(bit):
        return me + bit * (1 - 2 * lax.rem(lax.div(me, bit), 2))

    order = ((decay_hbm, decay_flat), (residue_hbm, residue_flat), (k_hbm, k_ref), (v_hbm, v_ref), (taps_hbm, taps_ref),
             (skip_hbm, skip_ref), (q_hbm, q_ref), (gain_hbm, gain_ref))
    tail_loads = [pltpu.make_async_copy(ref.at[tok - 16:tok, :], tails.at[j], tail_sem.at[j])
                  for j, ref in enumerate((q_hbm, k_hbm, v_hbm))]
    loads = [pltpu.make_async_copy(src, dst, load_sem.at[j]) for j, (src, dst) in enumerate(order)]
    for load in tail_loads + loads:
        load.start()
    barrier = pltpu.get_barrier_semaphore()
    for other in [right, left] + [partner(1 << r) for r in range(rounds)]:
        pl.semaphore_signal(barrier, inc=1, device_id={"seq": other}, device_id_type=MESH)
    for d in range(1, nch):
        pl.semaphore_signal(barrier, inc=1, device_id={"ch": lax.rem(mych + d, nch)}, device_id_type=MESH)

    halo_out[...] = jnp.zeros_like(halo_out)
    for j in range(3):
        tail_loads[j].wait()
        halo_out[2 * j:2 * j + 2, :] = tails[j].astype(f32)[14:16]
    pl.semaphore_wait(barrier, 2 + rounds + nch - 1)

    halo = pltpu.make_async_remote_copy(halo_out, halo_in, halo_send, halo_recv,
                                        device_id={"seq": right}, device_id_type=MESH)

    @pl.when(me < n - 1)
    def _():
        halo.start()

    lane = lax.broadcasted_iota(jnp.int32, (1, LANES), 1)
    lane_group = lane // modes
    lags_rev = (tok - 1 - lax.broadcasted_iota(jnp.int32, (1, tok), 1)).astype(f32)

    spread = (lax.broadcasted_iota(jnp.int32, (modes, LANES), 1) % modes
              == lax.broadcasted_iota(jnp.int32, (modes, LANES), 0)).astype(f32)
    after = (lax.broadcasted_iota(jnp.int32, (tok, 1), 0) + 1).astype(f32)
    sub = lax.broadcasted_iota(jnp.int32, (per, LANES), 0)
    sub_lane = lax.broadcasted_iota(jnp.int32, (per, LANES), 1) // modes

    def prepare(i, _):
        logs = decay_ref[pl.ds(pl.multiple_of(i * per, per), per), :]
        res = residue_ref[pl.ds(pl.multiple_of(i * per, per), per), :]
        pole = jnp.exp(logs)
        weight = res * jnp.sqrt(1.0 - pole * pole)
        cols, wcols = logs.T, weight.T
        rows = []
        wide_rate = jnp.zeros((modes, LANES), f32)
        wide_w = jnp.zeros((modes, LANES), f32)
        for j in range(per):
            col, wcol = cols[:, j:j + 1], wcols[:, j:j + 1]
            power = jnp.exp(col * lags_rev)
            leaving[pl.ds(pl.multiple_of(i * LANES, LANES) + j * modes, modes), :] = power.astype(bf16)
            rows.append(jnp.sum(power * wcol, axis=0, keepdims=True))
            wide_rate = jnp.where(lane_group == j, col, wide_rate)
            wide_w = jnp.where(lane_group == j, wcol, wide_w)
        hrev[pl.ds(pl.multiple_of(i * per, per), per), :] = jnp.concatenate(rows, axis=0)
        rate[:, tile_at(i)] = wide_rate
        wide_weight[:, tile_at(i)] = wide_w
        return 0

    loads[0].wait()
    loads[1].wait()
    decay_ref[...] = decay_flat[...].T
    residue_ref[...] = residue_flat[...].T
    lax.fori_loop(0, tiles, prepare, 0)
    for load in loads[2:6]:
        load.wait()

    @pl.when(me > 0)
    def _():
        halo.wait_recv()

    @pl.when(me == 0)
    def _():
        halo_in[...] = jnp.zeros_like(halo_in)

    def short(ref, which, i):
        pad[which, 8:8 + tok, :] = ref[:, tile_at(i)].astype(f32)
        pad[which, 0:8, :] = jnp.concatenate(
            [jnp.zeros((6, LANES), f32), halo_in[2 * which:2 * which + 2, tile_at(i)]], axis=0)
        a = [taps_ref[3 * which + t:3 * which + t + 1, tile_at(i)] for t in range(3)]
        return a[0] * pad[which, 8:8 + tok, :] + a[1] * pad[which, 7:7 + tok, :] + a[2] * pad[which, 6:6 + tok, :]

    def summarize(i, _):
        values = (short(k_ref, 1, i) * short(v_ref, 2, i)).astype(bf16)
        mixed[:, tile_at(i)] = values
        spreadout = jnp.dot(leaving[tile_at(i), :], values, preferred_element_type=f32)
        state = jnp.zeros((modes, LANES), f32)
        for j in range(per):
            state = jnp.where(lane_group == j, spreadout[j * modes:(j + 1) * modes], state)
        total[:, tile_at(i)] = state
        state_out[0, :, tile_at(i)] = state.astype(bf16)
        carry[:, tile_at(i)] = jnp.zeros((modes, LANES), f32)
        return 0

    lax.fori_loop(0, tiles, summarize, 0)

    causal = (lax.broadcasted_iota(jnp.int32, (half, tok), 1)
              <= lax.broadcasted_iota(jnp.int32, (half, tok), 0) + half)

    def convolve(i, _):
        values = mixed[:, tile_at(i)]
        first, second = values[:half], values[half:]
        right_side = jnp.concatenate(
            [jnp.concatenate([jnp.zeros_like(first), first], axis=1),
             jnp.concatenate([first, second], axis=1)], axis=0)
        lines = hrev[pl.ds(pl.multiple_of(i * per, per), per), :]
        blocks = []
        for j in range(per):
            line = jnp.broadcast_to(lines[j:j + 1], (half, tok))
            block = pltpu.roll(line, half + 1, 1, stride=1, stride_axis=0)
            blocks.append(jnp.where(causal, block, 0.0).astype(bf16))
        product = jnp.dot(jnp.concatenate(blocks, axis=0), right_side, preferred_element_type=f32)
        low = jnp.zeros((half, LANES), f32)
        high = jnp.zeros((half, LANES), f32)
        for j in range(per):
            part = product[j * half:(j + 1) * half]
            low = jnp.where(lane_group == j, part[:, :LANES], low)
            high = jnp.where(lane_group == j, part[:, LANES:], high)
        skip = skip_ref[:, tile_at(i)]
        conv[:half, tile_at(i)] = low + skip * first.astype(f32)
        conv[half:, tile_at(i)] = high + skip * second.astype(f32)
        logs = decay_ref[pl.ds(pl.multiple_of(i * per, per), per), :]
        row = jnp.dot(logs, spread, preferred_element_type=f32, precision=lax.Precision.HIGHEST)
        row = jnp.sum(jnp.where(sub == sub_lane, row, 0.0), axis=0, keepdims=True)
        entering[:, tile_at(i)] = jnp.exp(after * row).astype(bf16)
        return 0

    for r in range(rounds):
        bit = 1 << r
        last = r == rounds - 1
        upper = lax.rem(lax.div(me, bit), 2) == 1
        copy = pltpu.make_async_remote_copy(state_out.at[r], state_in.at[r], state_send.at[r], state_recv.at[r],
                                            device_id={"seq": partner(bit)}, device_id_type=MESH)
        if last:
            @pl.when(jnp.logical_not(upper))
            def _():
                copy.start()
        else:
            copy.start()
        lax.fori_loop(tiles * r // rounds, tiles * (r + 1) // rounds, convolve, 0)
        block_rate = float(tok * bit)
        offset = (lax.rem(me, bit) * tok).astype(f32)

        def merge(i, _):
            theirs = state_in[r, :, tile_at(i)].astype(f32)
            logs = rate[:, tile_at(i)]
            inward = jnp.exp(logs * offset) * theirs
            carry[:, tile_at(i)] += jnp.where(upper, inward, 0.0)
            if not last:
                mine = total[:, tile_at(i)]
                later = jnp.where(upper, mine, theirs)
                before = jnp.where(upper, theirs, mine)
                both = jnp.exp(logs * block_rate) * before + later
                total[:, tile_at(i)] = both
                state_out[r + 1, :, tile_at(i)] = both.astype(bf16)
            return 0

        if last:
            @pl.when(upper)
            def _():
                copy.wait_recv()
                lax.fori_loop(0, tiles, merge, 0)
        else:
            copy.wait_recv()
            lax.fori_loop(0, tiles, merge, 0)

    square[...] = jnp.zeros_like(square)
    loads[6].wait()
    loads[7].wait()

    def gate(i, _):
        state = carry[:, tile_at(i)] * wide_weight[:, tile_at(i)]
        diagonal = jnp.concatenate([jnp.where(lane_group == j, state, 0.0) for j in range(per)], axis=0)
        fine = diagonal.astype(bf16)
        rest = (diagonal - fine.astype(f32)).astype(bf16)
        ent = entering[:, tile_at(i)]
        carried = jnp.dot(jnp.concatenate([ent, ent], axis=1), jnp.concatenate([fine, rest], axis=0),
                          preferred_element_type=f32)
        q_short = short(q_ref, 0, i).astype(bf16).astype(f32)
        gated = q_short * (conv[:, tile_at(i)] + carried)
        conv[:, tile_at(i)] = gated
        square[...] += gated * gated
        return 0

    lax.fori_loop(0, tiles, gate, 0)

    sums = jnp.sum(square[...].T, axis=0, keepdims=True)
    square_out[...] = jnp.broadcast_to(sums, square_out.shape)
    copies = []
    for d in range(1, nch):
        c = pltpu.make_async_remote_copy(square_out, square_in.at[d - 1], square_send.at[d - 1], square_recv.at[d - 1],
                                         device_id={"ch": lax.rem(mych + d, nch)}, device_id_type=MESH)
        c.start()
        copies.append(c)
    for d, c in enumerate(copies):
        c.wait()
        sums = sums + square_in[d, 0:1, :]
    scale = lax.rsqrt(sums / (channels * nch) + 1e-5)
    square[...] = jnp.broadcast_to(scale, (LANES, tok)).T

    def finish(i, _):
        out_ref[:, tile_at(i)] = (conv[:, tile_at(i)] * square[...] * gain_ref[:, tile_at(i)]).astype(bf16)
        return 0

    lax.fori_loop(0, tiles, finish, 0)

    @pl.when(me < n - 1)
    def _():
        halo.wait_send()

    for r in range(rounds):
        bit = 1 << r
        copy = pltpu.make_async_remote_copy(state_out.at[r], state_in.at[r], state_send.at[r], state_recv.at[r],
                                            device_id={"seq": partner(bit)}, device_id_type=MESH)
        if r == rounds - 1:
            @pl.when(lax.rem(lax.div(me, bit), 2) == 0)
            def _():
                copy.wait_send()
        else:
            copy.wait_send()


def on_device(n, nch, q_proj, k_proj, v_proj, short_filter, log_decay, residue, skip_bias, norm_gain):
    tok, channels = q_proj.shape
    groups, modes = log_decay.shape
    rounds = n.bit_length() - 1
    assert n == 1 << rounds and channels == groups * modes
    vmem = pl.BlockSpec(memory_space=pltpu.VMEM)
    dma = pltpu.SemaphoreType.DMA
    return pl.pallas_call(
        functools.partial(kernel, n, nch, rounds, modes),
        out_shape=jax.ShapeDtypeStruct((tok, channels), bf16),
        in_specs=[pl.BlockSpec(memory_space=pltpu.HBM)] * 8,
        out_specs=vmem,
        scratch_shapes=[
            pltpu.VMEM((tok, channels), bf16),
            pltpu.VMEM((tok, channels), bf16),
            pltpu.VMEM((tok, channels), bf16),
            pltpu.VMEM((9, channels), f32),
            pltpu.VMEM((modes, groups), f32),
            pltpu.VMEM((modes, groups), f32),
            pltpu.VMEM((1, channels), f32),
            pltpu.VMEM((1, channels), f32),
            pltpu.VMEM((3, 16, channels), bf16),
            pltpu.VMEM((groups, modes), f32),
            pltpu.VMEM((groups, modes), f32),
            pltpu.VMEM((8, channels), f32),
            pltpu.VMEM((8, channels), f32),
            pltpu.VMEM((3, tok + 8, LANES), f32),
            pltpu.VMEM((channels, tok), bf16),
            pltpu.VMEM((groups, tok), f32),
            pltpu.VMEM((tok, channels), bf16),
            pltpu.VMEM((tok, channels), bf16),
            pltpu.VMEM((tok, channels), f32),
            pltpu.VMEM((modes, channels), f32),
            pltpu.VMEM((modes, channels), f32),
            pltpu.VMEM((modes, channels), f32),
            pltpu.VMEM((modes, channels), f32),
            pltpu.VMEM((rounds, modes, channels), bf16),
            pltpu.VMEM((rounds, modes, channels), bf16),
            pltpu.VMEM((tok, LANES), f32),
            pltpu.VMEM((8, tok), f32),
            pltpu.VMEM((max(nch - 1, 1), 8, tok), f32),
            dma, dma, dma((rounds,)), dma((rounds,)), dma((max(nch - 1, 1),)), dma((max(nch - 1, 1),)),
            dma((8,)), dma((3,)),
        ],
        compiler_params=pltpu.CompilerParams(collective_id=0, has_side_effects=True,
                                             vmem_limit_bytes=50 * 1024 * 1024),
    )(q_proj, k_proj, v_proj, short_filter, log_decay.T, residue.T,
      skip_bias.reshape(1, channels), norm_gain.reshape(1, channels))


def solution(mesh):
    return jax.shard_map(
        functools.partial(on_device, mesh.shape["seq"], mesh.shape["ch"]),
        mesh=mesh,
        in_specs=(P("seq", "ch"), P("seq", "ch"), P("seq", "ch"), P(None, "ch"),
                  P("ch", None), P("ch", None), P("ch"), P("ch")),
        out_specs=P("seq", "ch"),
        check_vma=False,
    )
```

```python
import functools
import jax
import jax.numpy as jnp
from jax import lax
from jax.experimental import pallas as pl
from jax.experimental.pallas import tpu as pltpu
from jax.sharding import PartitionSpec as P

LANES = 128
MESH = pl.DeviceIdType.MESH
f32 = jnp.float32
bf16 = jnp.bfloat16


def tile_at(i):
    return pl.ds(pl.multiple_of(i * LANES, LANES), LANES)


def kernel(n, nch, rounds, modes, q_hbm, k_hbm, v_hbm, taps_hbm, decay_hbm, residue_hbm, skip_hbm, gain_hbm,
           out_ref, q_ref, k_ref, v_ref, taps_ref, decay_flat, residue_flat, skip_ref, gain_ref,
           tails, decay_ref, residue_ref, halo_out, halo_in, pad, leaving, hrev, entering, mixed, conv, rate, wide_weight,
           total, carry, state_out, state_in, square, square_out, square_in,
           halo_send, halo_recv, state_send, state_recv, square_send, square_recv, load_sem, tail_sem):
    tok, channels = q_ref.shape
    half = tok // 2
    tiles = channels // LANES
    per = LANES // modes
    me = lax.axis_index("seq")
    mych = lax.axis_index("ch")
    right, left = lax.rem(me + 1, n), lax.rem(me + n - 1, n)

    def partner(bit):
        return me + bit * (1 - 2 * lax.rem(lax.div(me, bit), 2))

    order = ((decay_hbm, decay_flat), (residue_hbm, residue_flat), (k_hbm, k_ref), (v_hbm, v_ref), (taps_hbm, taps_ref),
             (skip_hbm, skip_ref), (q_hbm, q_ref), (gain_hbm, gain_ref))
    tail_loads = [pltpu.make_async_copy(ref.at[tok - 16:tok, :], tails.at[j], tail_sem.at[j])
                  for j, ref in enumerate((q_hbm, k_hbm, v_hbm))]
    loads = [pltpu.make_async_copy(src, dst, load_sem.at[j]) for j, (src, dst) in enumerate(order)]
    for load in tail_loads + loads:
        load.start()
    barrier = pltpu.get_barrier_semaphore()
    for other in [right, left] + [partner(1 << r) for r in range(rounds)]:
        pl.semaphore_signal(barrier, inc=1, device_id={"seq": other}, device_id_type=MESH)
    for d in range(1, nch):
        pl.semaphore_signal(barrier, inc=1, device_id={"ch": lax.rem(mych + d, nch)}, device_id_type=MESH)

    halo_out[...] = jnp.zeros_like(halo_out)
    for j in range(3):
        tail_loads[j].wait()
        halo_out[2 * j:2 * j + 2, :] = tails[j].astype(f32)[14:16]
    pl.semaphore_wait(barrier, 2 + rounds + nch - 1)

    halo = pltpu.make_async_remote_copy(halo_out, halo_in, halo_send, halo_recv,
                                        device_id={"seq": right}, device_id_type=MESH)

    @pl.when(me < n - 1)
    def _():
        halo.start()

    lane = lax.broadcasted_iota(jnp.int32, (1, LANES), 1)
    lane_group = lane // modes
    lags_rev = (tok - 1 - lax.broadcasted_iota(jnp.int32, (1, tok), 1)).astype(f32)

    spread = (lax.broadcasted_iota(jnp.int32, (modes, LANES), 1) % modes
              == lax.broadcasted_iota(jnp.int32, (modes, LANES), 0)).astype(f32)
    after = (lax.broadcasted_iota(jnp.int32, (tok, 1), 0) + 1).astype(f32)
    sub = lax.broadcasted_iota(jnp.int32, (per, LANES), 0)
    sub_lane = lax.broadcasted_iota(jnp.int32, (per, LANES), 1) // modes

    def prepare(i, _):
        logs = decay_ref[pl.ds(pl.multiple_of(i * per, per), per), :]
        res = residue_ref[pl.ds(pl.multiple_of(i * per, per), per), :]
        pole = jnp.exp(logs)
        weight = res * jnp.sqrt(1.0 - pole * pole)
        cols, wcols = logs.T, weight.T
        rows = []
        wide_rate = jnp.zeros((modes, LANES), f32)
        wide_w = jnp.zeros((modes, LANES), f32)
        for j in range(per):
            col, wcol = cols[:, j:j + 1], wcols[:, j:j + 1]
            power = jnp.exp(col * lags_rev)
            leaving[pl.ds(pl.multiple_of(i * LANES, LANES) + j * modes, modes), :] = power.astype(bf16)
            rows.append(jnp.sum(power * wcol, axis=0, keepdims=True))
            wide_rate = jnp.where(lane_group == j, col, wide_rate)
            wide_w = jnp.where(lane_group == j, wcol, wide_w)
        hrev[pl.ds(pl.multiple_of(i * per, per), per), :] = jnp.concatenate(rows, axis=0)
        rate[:, tile_at(i)] = wide_rate
        wide_weight[:, tile_at(i)] = wide_w
        return 0

    loads[0].wait()
    loads[1].wait()
    decay_ref[...] = decay_flat[...].T
    residue_ref[...] = residue_flat[...].T
    lax.fori_loop(0, tiles, prepare, 0)
    for load in loads[2:6]:
        load.wait()

    @pl.when(me > 0)
    def _():
        halo.wait_recv()

    @pl.when(me == 0)
    def _():
        halo_in[...] = jnp.zeros_like(halo_in)

    def short(ref, which, i):
        pad[which, 8:8 + tok, :] = ref[:, tile_at(i)].astype(f32)
        pad[which, 0:8, :] = jnp.concatenate(
            [jnp.zeros((6, LANES), f32), halo_in[2 * which:2 * which + 2, tile_at(i)]], axis=0)
        a = [taps_ref[3 * which + t:3 * which + t + 1, tile_at(i)] for t in range(3)]
        return a[0] * pad[which, 8:8 + tok, :] + a[1] * pad[which, 7:7 + tok, :] + a[2] * pad[which, 6:6 + tok, :]

    def summarize(i, _):
        values = (short(k_ref, 1, i) * short(v_ref, 2, i)).astype(bf16)
        mixed[:, tile_at(i)] = values
        spreadout = jnp.dot(leaving[tile_at(i), :], values, preferred_element_type=f32)
        state = jnp.zeros((modes, LANES), f32)
        for j in range(per):
            state = jnp.where(lane_group == j, spreadout[j * modes:(j + 1) * modes], state)
        total[:, tile_at(i)] = state
        state_out[0, :, tile_at(i)] = state.astype(bf16)
        carry[:, tile_at(i)] = jnp.zeros((modes, LANES), f32)
        return 0

    lax.fori_loop(0, tiles, summarize, 0)

    causal = (lax.broadcasted_iota(jnp.int32, (half, tok), 1)
              <= lax.broadcasted_iota(jnp.int32, (half, tok), 0) + half)

    def convolve(i, _):
        values = mixed[:, tile_at(i)]
        first, second = values[:half], values[half:]
        right_side = jnp.concatenate(
            [jnp.concatenate([jnp.zeros_like(first), first], axis=1),
             jnp.concatenate([first, second], axis=1)], axis=0)
        lines = hrev[pl.ds(pl.multiple_of(i * per, per), per), :]
        blocks = []
        for j in range(per):
            line = jnp.broadcast_to(lines[j:j + 1], (half, tok))
            block = pltpu.roll(line, half + 1, 1, stride=1, stride_axis=0)
            blocks.append(jnp.where(causal, block, 0.0).astype(bf16))
        product = jnp.dot(jnp.concatenate(blocks, axis=0), right_side, preferred_element_type=f32)
        low = jnp.zeros((half, LANES), f32)
        high = jnp.zeros((half, LANES), f32)
        for j in range(per):
            part = product[j * half:(j + 1) * half]
            low = jnp.where(lane_group == j, part[:, :LANES], low)
            high = jnp.where(lane_group == j, part[:, LANES:], high)
        skip = skip_ref[:, tile_at(i)]
        conv[:half, tile_at(i)] = low + skip * first.astype(f32)
        conv[half:, tile_at(i)] = high + skip * second.astype(f32)
        logs = decay_ref[pl.ds(pl.multiple_of(i * per, per), per), :]
        row = jnp.dot(logs, spread, preferred_element_type=f32, precision=lax.Precision.HIGHEST)
        row = jnp.sum(jnp.where(sub == sub_lane, row, 0.0), axis=0, keepdims=True)
        entering[:, tile_at(i)] = jnp.exp(after * row).astype(bf16)
        q_ref[:, tile_at(i)] = short(q_ref, 0, i).astype(bf16)
        return 0

    loads[6].wait()

    for r in range(rounds):
        bit = 1 << r
        last = r == rounds - 1
        upper = lax.rem(lax.div(me, bit), 2) == 1
        copy = pltpu.make_async_remote_copy(state_out.at[r], state_in.at[r], state_send.at[r], state_recv.at[r],
                                            device_id={"seq": partner(bit)}, device_id_type=MESH)
        if last:
            @pl.when(jnp.logical_not(upper))
            def _():
                copy.start()
        else:
            copy.start()
        lax.fori_loop(tiles * r // rounds, tiles * (r + 1) // rounds, convolve, 0)
        block_rate = float(tok * bit)
        offset = (lax.rem(me, bit) * tok).astype(f32)

        def merge(i, _):
            theirs = state_in[r, :, tile_at(i)].astype(f32)
            logs = rate[:, tile_at(i)]
            inward = jnp.exp(logs * offset) * theirs
            carry[:, tile_at(i)] += jnp.where(upper, inward, 0.0)
            if not last:
                mine = total[:, tile_at(i)]
                later = jnp.where(upper, mine, theirs)
                before = jnp.where(upper, theirs, mine)
                both = jnp.exp(logs * block_rate) * before + later
                total[:, tile_at(i)] = both
                state_out[r + 1, :, tile_at(i)] = both.astype(bf16)
            return 0

        if last:
            @pl.when(upper)
            def _():
                copy.wait_recv()
                lax.fori_loop(0, tiles, merge, 0)
        else:
            copy.wait_recv()
            lax.fori_loop(0, tiles, merge, 0)

    square[...] = jnp.zeros_like(square)
    loads[7].wait()

    def gate(i, _):
        state = carry[:, tile_at(i)] * wide_weight[:, tile_at(i)]
        diagonal = jnp.concatenate([jnp.where(lane_group == j, state, 0.0) for j in range(per)], axis=0)
        fine = diagonal.astype(bf16)
        rest = (diagonal - fine.astype(f32)).astype(bf16)
        ent = entering[:, tile_at(i)]
        carried = jnp.dot(jnp.concatenate([ent, ent], axis=1), jnp.concatenate([fine, rest], axis=0),
                          preferred_element_type=f32)
        q_short = q_ref[:, tile_at(i)].astype(f32)
        gated = q_short * (conv[:, tile_at(i)] + carried)
        conv[:, tile_at(i)] = gated
        square[...] += gated * gated
        return 0

    lax.fori_loop(0, tiles, gate, 0)

    sums = jnp.sum(square[...].T, axis=0, keepdims=True)
    square_out[...] = jnp.broadcast_to(sums, square_out.shape)
    copies = []
    for d in range(1, nch):
        c = pltpu.make_async_remote_copy(square_out, square_in.at[d - 1], square_send.at[d - 1], square_recv.at[d - 1],
                                         device_id={"ch": lax.rem(mych + d, nch)}, device_id_type=MESH)
        c.start()
        copies.append(c)
    for d, c in enumerate(copies):
        c.wait()
        sums = sums + square_in[d, 0:1, :]
    scale = lax.rsqrt(sums / (channels * nch) + 1e-5)
    square[...] = jnp.broadcast_to(scale, (LANES, tok)).T

    def finish(i, _):
        out_ref[:, tile_at(i)] = (conv[:, tile_at(i)] * square[...] * gain_ref[:, tile_at(i)]).astype(bf16)
        return 0

    lax.fori_loop(0, tiles, finish, 0)

    @pl.when(me < n - 1)
    def _():
        halo.wait_send()

    for r in range(rounds):
        bit = 1 << r
        copy = pltpu.make_async_remote_copy(state_out.at[r], state_in.at[r], state_send.at[r], state_recv.at[r],
                                            device_id={"seq": partner(bit)}, device_id_type=MESH)
        if r == rounds - 1:
            @pl.when(lax.rem(lax.div(me, bit), 2) == 0)
            def _():
                copy.wait_send()
        else:
            copy.wait_send()


def on_device(n, nch, q_proj, k_proj, v_proj, short_filter, log_decay, residue, skip_bias, norm_gain):
    tok, channels = q_proj.shape
    groups, modes = log_decay.shape
    rounds = n.bit_length() - 1
    assert n == 1 << rounds and channels == groups * modes
    vmem = pl.BlockSpec(memory_space=pltpu.VMEM)
    dma = pltpu.SemaphoreType.DMA
    return pl.pallas_call(
        functools.partial(kernel, n, nch, rounds, modes),
        out_shape=jax.ShapeDtypeStruct((tok, channels), bf16),
        in_specs=[pl.BlockSpec(memory_space=pltpu.HBM)] * 8,
        out_specs=vmem,
        scratch_shapes=[
            pltpu.VMEM((tok, channels), bf16),
            pltpu.VMEM((tok, channels), bf16),
            pltpu.VMEM((tok, channels), bf16),
            pltpu.VMEM((9, channels), f32),
            pltpu.VMEM((modes, groups), f32),
            pltpu.VMEM((modes, groups), f32),
            pltpu.VMEM((1, channels), f32),
            pltpu.VMEM((1, channels), f32),
            pltpu.VMEM((3, 16, channels), bf16),
            pltpu.VMEM((groups, modes), f32),
            pltpu.VMEM((groups, modes), f32),
            pltpu.VMEM((8, channels), f32),
            pltpu.VMEM((8, channels), f32),
            pltpu.VMEM((3, tok + 8, LANES), f32),
            pltpu.VMEM((channels, tok), bf16),
            pltpu.VMEM((groups, tok), f32),
            pltpu.VMEM((tok, channels), bf16),
            pltpu.VMEM((tok, channels), bf16),
            pltpu.VMEM((tok, channels), f32),
            pltpu.VMEM((modes, channels), f32),
            pltpu.VMEM((modes, channels), f32),
            pltpu.VMEM((modes, channels), f32),
            pltpu.VMEM((modes, channels), f32),
            pltpu.VMEM((rounds, modes, channels), bf16),
            pltpu.VMEM((rounds, modes, channels), bf16),
            pltpu.VMEM((tok, LANES), f32),
            pltpu.VMEM((8, tok), f32),
            pltpu.VMEM((max(nch - 1, 1), 8, tok), f32),
            dma, dma, dma((rounds,)), dma((rounds,)), dma((max(nch - 1, 1),)), dma((max(nch - 1, 1),)),
            dma((8,)), dma((3,)),
        ],
        compiler_params=pltpu.CompilerParams(collective_id=0, has_side_effects=True,
                                             vmem_limit_bytes=50 * 1024 * 1024),
    )(q_proj, k_proj, v_proj, short_filter, log_decay.T, residue.T,
      skip_bias.reshape(1, channels), norm_gain.reshape(1, channels))


def solution(mesh):
    return jax.shard_map(
        functools.partial(on_device, mesh.shape["seq"], mesh.shape["ch"]),
        mesh=mesh,
        in_specs=(P("seq", "ch"), P("seq", "ch"), P("seq", "ch"), P(None, "ch"),
                  P("ch", None), P("ch", None), P("ch"), P("ch")),
        out_specs=P("seq", "ch"),
        check_vma=False,
    )
```

```python
import functools
import jax
import jax.numpy as jnp
from jax import lax
from jax.experimental import pallas as pl
from jax.experimental.pallas import tpu as pltpu
from jax.sharding import PartitionSpec as P

LANES = 128
MESH = pl.DeviceIdType.MESH
f32 = jnp.float32
bf16 = jnp.bfloat16


def tile_at(i):
    return pl.ds(pl.multiple_of(i * LANES, LANES), LANES)


def kernel(n, nch, rounds, modes, q_hbm, k_hbm, v_hbm, taps_hbm, decay_hbm, residue_hbm, skip_hbm, gain_hbm,
           out_ref, q_ref, k_ref, v_ref, taps_ref, decay_flat, residue_flat, skip_ref, gain_ref,
           tails, decay_ref, residue_ref, halo_out, halo_in, pad, leaving, hrev, entering, mixed, conv, rate, wide_weight,
           total, carry, carry_in, first_out, first_in, state_out, state_in, square, square_out, square_in,
           halo_send, halo_recv, state_send, state_recv, square_send, square_recv, load_sem, tail_sem, carry_send, carry_recv):
    tok, channels = q_ref.shape
    half = tok // 2
    tiles = channels // LANES
    per = LANES // modes
    me = lax.axis_index("seq")
    mych = lax.axis_index("ch")
    right, left = lax.rem(me + 1, n), lax.rem(me + n - 1, n)

    def partner(bit):
        return me + bit * (1 - 2 * lax.rem(lax.div(me, bit), 2))

    def scan_copy(r):
        return pltpu.make_async_remote_copy(
            state_out.at[r] if r else first_out, state_in.at[r] if r else first_in, state_send.at[r], state_recv.at[r],
            device_id={"seq": partner(1 << r)}, device_id_type=MESH)

    order = ((decay_hbm, decay_flat), (residue_hbm, residue_flat), (k_hbm, k_ref), (v_hbm, v_ref), (taps_hbm, taps_ref),
             (skip_hbm, skip_ref), (q_hbm, q_ref), (gain_hbm, gain_ref))
    tail_loads = [pltpu.make_async_copy(ref.at[tok - 16:tok, :], tails.at[j], tail_sem.at[j])
                  for j, ref in enumerate((q_hbm, k_hbm, v_hbm))]
    loads = [pltpu.make_async_copy(src, dst, load_sem.at[j]) for j, (src, dst) in enumerate(order)]
    for load in tail_loads + loads:
        load.start()
    barrier = pltpu.get_barrier_semaphore()
    for other in [right, left] + [partner(1 << r) for r in range(rounds)]:
        pl.semaphore_signal(barrier, inc=1, device_id={"seq": other}, device_id_type=MESH)
    for d in range(1, nch):
        pl.semaphore_signal(barrier, inc=1, device_id={"ch": lax.rem(mych + d, nch)}, device_id_type=MESH)

    halo_out[...] = jnp.zeros_like(halo_out)
    for j in range(3):
        tail_loads[j].wait()
        halo_out[2 * j:2 * j + 2, :] = tails[j].astype(f32)[14:16]
    pl.semaphore_wait(barrier, 2 + rounds + nch - 1)

    halo = pltpu.make_async_remote_copy(halo_out, halo_in, halo_send, halo_recv,
                                        device_id={"seq": right}, device_id_type=MESH)

    @pl.when(me < n - 1)
    def _():
        halo.start()

    lane = lax.broadcasted_iota(jnp.int32, (1, LANES), 1)
    lane_group = lane // modes
    lags_rev = (tok - 1 - lax.broadcasted_iota(jnp.int32, (1, tok), 1)).astype(f32)

    spread = (lax.broadcasted_iota(jnp.int32, (modes, LANES), 1) % modes
              == lax.broadcasted_iota(jnp.int32, (modes, LANES), 0)).astype(f32)
    after = (lax.broadcasted_iota(jnp.int32, (tok, 1), 0) + 1).astype(f32)
    sub = lax.broadcasted_iota(jnp.int32, (per, LANES), 0)
    sub_lane = lax.broadcasted_iota(jnp.int32, (per, LANES), 1) // modes

    def prepare(i, _):
        logs = decay_ref[pl.ds(pl.multiple_of(i * per, per), per), :]
        res = residue_ref[pl.ds(pl.multiple_of(i * per, per), per), :]
        pole = jnp.exp(logs)
        weight = res * jnp.sqrt(1.0 - pole * pole)
        cols, wcols = logs.T, weight.T
        rows = []
        wide_rate = jnp.zeros((modes, LANES), f32)
        wide_w = jnp.zeros((modes, LANES), f32)
        for j in range(per):
            col, wcol = cols[:, j:j + 1], wcols[:, j:j + 1]
            power = jnp.exp(col * lags_rev)
            leaving[pl.ds(pl.multiple_of(i * LANES, LANES) + j * modes, modes), :] = power.astype(bf16)
            rows.append(jnp.sum(power * wcol, axis=0, keepdims=True))
            wide_rate = jnp.where(lane_group == j, col, wide_rate)
            wide_w = jnp.where(lane_group == j, wcol, wide_w)
        hrev[pl.ds(pl.multiple_of(i * per, per), per), :] = jnp.concatenate(rows, axis=0)
        rate[:, tile_at(i)] = wide_rate
        wide_weight[:, tile_at(i)] = wide_w
        return 0

    loads[0].wait()
    loads[1].wait()
    decay_ref[...] = decay_flat[...].T
    residue_ref[...] = residue_flat[...].T
    lax.fori_loop(0, tiles, prepare, 0)
    for load in loads[2:6]:
        load.wait()

    @pl.when(me > 0)
    def _():
        halo.wait_recv()

    @pl.when(me == 0)
    def _():
        halo_in[...] = jnp.zeros_like(halo_in)

    def short(ref, which, i):
        pad[which, 8:8 + tok, :] = ref[:, tile_at(i)].astype(f32)
        pad[which, 0:8, :] = jnp.concatenate(
            [jnp.zeros((6, LANES), f32), halo_in[2 * which:2 * which + 2, tile_at(i)]], axis=0)
        a = [taps_ref[3 * which + t:3 * which + t + 1, tile_at(i)] for t in range(3)]
        return a[0] * pad[which, 8:8 + tok, :] + a[1] * pad[which, 7:7 + tok, :] + a[2] * pad[which, 6:6 + tok, :]

    def summarize(i, _):
        values = (short(k_ref, 1, i) * short(v_ref, 2, i)).astype(bf16)
        mixed[:, tile_at(i)] = values
        spreadout = jnp.dot(leaving[tile_at(i), :], values, preferred_element_type=f32)
        state = jnp.zeros((modes, LANES), f32)
        for j in range(per):
            state = jnp.where(lane_group == j, spreadout[j * modes:(j + 1) * modes], state)
        total[:, tile_at(i)] = state
        first_out[:, tile_at(i)] = state.astype(bf16)
        return 0

    lax.fori_loop(0, tiles, summarize, 0)

    causal = (lax.broadcasted_iota(jnp.int32, (half, tok), 1)
              <= lax.broadcasted_iota(jnp.int32, (half, tok), 0) + half)

    def convolve(i, _):
        values = mixed[:, tile_at(i)]
        first, second = values[:half], values[half:]
        right_side = jnp.concatenate(
            [jnp.concatenate([jnp.zeros_like(first), first], axis=1),
             jnp.concatenate([first, second], axis=1)], axis=0)
        lines = hrev[pl.ds(pl.multiple_of(i * per, per), per), :]
        blocks = []
        for j in range(per):
            line = jnp.broadcast_to(lines[j:j + 1], (half, tok))
            block = pltpu.roll(line, half + 1, 1, stride=1, stride_axis=0)
            blocks.append(jnp.where(causal, block, 0.0).astype(bf16))
        product = jnp.dot(jnp.concatenate(blocks, axis=0), right_side, preferred_element_type=f32)
        low = jnp.zeros((half, LANES), f32)
        high = jnp.zeros((half, LANES), f32)
        for j in range(per):
            part = product[j * half:(j + 1) * half]
            low = jnp.where(lane_group == j, part[:, :LANES], low)
            high = jnp.where(lane_group == j, part[:, LANES:], high)
        skip = skip_ref[:, tile_at(i)]
        conv[:half, tile_at(i)] = low + skip * first.astype(f32)
        conv[half:, tile_at(i)] = high + skip * second.astype(f32)
        logs = decay_ref[pl.ds(pl.multiple_of(i * per, per), per), :]
        row = jnp.dot(logs, spread, preferred_element_type=f32, precision=lax.Precision.HIGHEST)
        row = jnp.sum(jnp.where(sub == sub_lane, row, 0.0), axis=0, keepdims=True)
        entering[:, tile_at(i)] = jnp.exp(after * row).astype(bf16)
        q_ref[:, tile_at(i)] = short(q_ref, 0, i).astype(bf16)
        return 0

    loads[6].wait()

    carry[...] = jnp.zeros_like(carry)
    half_tiles = tiles // 2
    core = lax.rem(me, 2)
    lead = max(tiles // 8, 1)
    tail = max(tiles // 16, 1)
    bounds = [0] + [lead + (tiles - lead - tail) * r // (rounds - 1) for r in range(rounds)]
    for r in range(rounds):
        bit = 1 << r
        last = r == rounds - 1
        upper = lax.rem(lax.div(me, bit), 2) == 1
        copy = scan_copy(r)
        if last:
            @pl.when(jnp.logical_not(upper))
            def _():
                copy.start()
        else:
            copy.start()
        lax.fori_loop(bounds[r], bounds[r + 1], convolve, 0)
        block_rate = float(tok * bit)
        offset = ((lax.rem(me, bit) - core) * tok).astype(f32) if r else None

        def merge(i, _):
            place = tile_at(core * half_tiles + i)
            theirs = (state_in[r, :, tile_at(i)] if r else first_in[:, place]).astype(f32)
            logs = rate[:, place]
            if r:
                inward = jnp.exp(logs * offset) * theirs
                carry[:, tile_at(i)] += jnp.where(upper, inward, 0.0)
            if not last:
                mine = total[:, place]
                later = jnp.where(upper, mine, theirs)
                before = jnp.where(upper, theirs, mine)
                both = jnp.exp(logs * block_rate) * before + later
                total[:, place] = both
                state_out[r + 1, :, tile_at(i)] = both.astype(bf16)
            return 0

        if last:
            @pl.when(upper)
            def _():
                copy.wait_recv()
                lax.fori_loop(0, half_tiles, merge, 0)
        else:
            copy.wait_recv()
            lax.fori_loop(0, half_tiles, merge, 0)

    share = pltpu.make_async_remote_copy(carry, carry_in, carry_send, carry_recv,
                                         device_id={"seq": partner(1)}, device_id_type=MESH)
    share.start()
    lax.fori_loop(bounds[rounds], tiles, convolve, 0)
    share.wait()

    def assemble(i, _):
        for part, side in ((carry, core), (carry_in, 1 - core)):
            place = tile_at(side * half_tiles + i)
            entry = part[:, tile_at(i)]
            moved = jnp.exp(rate[:, place] * float(tok)) * entry + first_in[:, place].astype(f32)
            total[:, place] = jnp.where(core == 1, moved, entry)
        return 0

    lax.fori_loop(0, half_tiles, assemble, 0)

    square[...] = jnp.zeros_like(square)
    loads[7].wait()

    def gate(i, _):
        state = total[:, tile_at(i)] * wide_weight[:, tile_at(i)]
        diagonal = jnp.concatenate([jnp.where(lane_group == j, state, 0.0) for j in range(per)], axis=0)
        fine = diagonal.astype(bf16)
        rest = (diagonal - fine.astype(f32)).astype(bf16)
        ent = entering[:, tile_at(i)]
        carried = jnp.dot(jnp.concatenate([ent, ent], axis=1), jnp.concatenate([fine, rest], axis=0),
                          preferred_element_type=f32)
        q_short = q_ref[:, tile_at(i)].astype(f32)
        gated = q_short * (conv[:, tile_at(i)] + carried)
        conv[:, tile_at(i)] = gated
        square[...] += gated * gated
        return 0

    lax.fori_loop(0, tiles, gate, 0)

    sums = jnp.sum(square[...].T, axis=0, keepdims=True)
    square_out[...] = jnp.broadcast_to(sums, square_out.shape)
    copies = []
    for d in range(1, nch):
        c = pltpu.make_async_remote_copy(square_out, square_in.at[d - 1], square_send.at[d - 1], square_recv.at[d - 1],
                                         device_id={"ch": lax.rem(mych + d, nch)}, device_id_type=MESH)
        c.start()
        copies.append(c)
    for d, c in enumerate(copies):
        c.wait()
        sums = sums + square_in[d, 0:1, :]
    scale = lax.rsqrt(sums / (channels * nch) + 1e-5)
    square[...] = jnp.broadcast_to(scale, (LANES, tok)).T

    def finish(i, _):
        out_ref[:, tile_at(i)] = (conv[:, tile_at(i)] * square[...] * gain_ref[:, tile_at(i)]).astype(bf16)
        return 0

    lax.fori_loop(0, tiles, finish, 0)

    @pl.when(me < n - 1)
    def _():
        halo.wait_send()

    for r in range(rounds):
        bit = 1 << r
        copy = scan_copy(r)
        if r == rounds - 1:
            @pl.when(lax.rem(lax.div(me, bit), 2) == 0)
            def _():
                copy.wait_send()
        else:
            copy.wait_send()


def on_device(n, nch, q_proj, k_proj, v_proj, short_filter, log_decay, residue, skip_bias, norm_gain):
    tok, channels = q_proj.shape
    groups, modes = log_decay.shape
    rounds = n.bit_length() - 1
    assert n == 1 << rounds and rounds > 1 and channels == groups * modes
    vmem = pl.BlockSpec(memory_space=pltpu.VMEM)
    dma = pltpu.SemaphoreType.DMA
    return pl.pallas_call(
        functools.partial(kernel, n, nch, rounds, modes),
        out_shape=jax.ShapeDtypeStruct((tok, channels), bf16),
        in_specs=[pl.BlockSpec(memory_space=pltpu.HBM)] * 8,
        out_specs=vmem,
        scratch_shapes=[
            pltpu.VMEM((tok, channels), bf16),
            pltpu.VMEM((tok, channels), bf16),
            pltpu.VMEM((tok, channels), bf16),
            pltpu.VMEM((9, channels), f32),
            pltpu.VMEM((modes, groups), f32),
            pltpu.VMEM((modes, groups), f32),
            pltpu.VMEM((1, channels), f32),
            pltpu.VMEM((1, channels), f32),
            pltpu.VMEM((3, 16, channels), bf16),
            pltpu.VMEM((groups, modes), f32),
            pltpu.VMEM((groups, modes), f32),
            pltpu.VMEM((8, channels), f32),
            pltpu.VMEM((8, channels), f32),
            pltpu.VMEM((3, tok + 8, LANES), f32),
            pltpu.VMEM((channels, tok), bf16),
            pltpu.VMEM((groups, tok), f32),
            pltpu.VMEM((tok, channels), bf16),
            pltpu.VMEM((tok, channels), bf16),
            pltpu.VMEM((tok, channels), f32),
            pltpu.VMEM((modes, channels), f32),
            pltpu.VMEM((modes, channels), f32),
            pltpu.VMEM((modes, channels), f32),
            pltpu.VMEM((modes, channels // 2), f32),
            pltpu.VMEM((modes, channels // 2), f32),
            pltpu.VMEM((modes, channels), bf16),
            pltpu.VMEM((modes, channels), bf16),
            pltpu.VMEM((rounds, modes, channels // 2), bf16),
            pltpu.VMEM((rounds, modes, channels // 2), bf16),
            pltpu.VMEM((tok, LANES), f32),
            pltpu.VMEM((8, tok), f32),
            pltpu.VMEM((max(nch - 1, 1), 8, tok), f32),
            dma, dma, dma((rounds,)), dma((rounds,)), dma((max(nch - 1, 1),)), dma((max(nch - 1, 1),)),
            dma((8,)), dma((3,)), dma, dma,
        ],
        compiler_params=pltpu.CompilerParams(collective_id=0, has_side_effects=True,
                                             vmem_limit_bytes=50 * 1024 * 1024),
    )(q_proj, k_proj, v_proj, short_filter, log_decay.T, residue.T,
      skip_bias.reshape(1, channels), norm_gain.reshape(1, channels))


def solution(mesh):
    return jax.shard_map(
        functools.partial(on_device, mesh.shape["seq"], mesh.shape["ch"]),
        mesh=mesh,
        in_specs=(P("seq", "ch"), P("seq", "ch"), P("seq", "ch"), P(None, "ch"),
                  P("ch", None), P("ch", None), P("ch"), P("ch")),
        out_specs=P("seq", "ch"),
        check_vma=False,
    )
```

```python
import functools
import jax
import jax.numpy as jnp
from jax import lax
from jax.experimental import pallas as pl
from jax.experimental.pallas import tpu as pltpu
from jax.sharding import PartitionSpec as P

LANES = 128
MESH = pl.DeviceIdType.MESH
f32 = jnp.float32
bf16 = jnp.bfloat16


def tile_at(i):
    return pl.ds(pl.multiple_of(i * LANES, LANES), LANES)


def kernel(n, nch, rounds, modes, q_hbm, k_hbm, v_hbm, taps_hbm, decay_hbm, residue_hbm, skip_hbm, gain_hbm,
           out_ref, q_ref, k_ref, v_ref, taps_ref, decay_flat, residue_flat, skip_ref, gain_ref,
           tails, decay_ref, residue_ref, halo_out, halo_in, pad, leaving, hrev, entering, mixed, conv, rate, wide_weight,
           total, carry, carry_in, first_out, first_in, state_out, state_in, square, square_out, square_in,
           halo_send, halo_recv, state_send, state_recv, square_send, square_recv, load_sem, tail_sem, carry_send, carry_recv):
    tok, channels = q_ref.shape
    half = tok // 2
    tiles = channels // LANES
    per = LANES // modes
    me = lax.axis_index("seq")
    mych = lax.axis_index("ch")
    right, left = lax.rem(me + 1, n), lax.rem(me + n - 1, n)

    def partner(bit):
        return me + bit * (1 - 2 * lax.rem(lax.div(me, bit), 2))

    def scan_copy(r):
        return pltpu.make_async_remote_copy(
            state_out.at[r] if r else first_out, state_in.at[r] if r else first_in, state_send.at[r], state_recv.at[r],
            device_id={"seq": partner(1 << r)}, device_id_type=MESH)

    order = ((decay_hbm, decay_flat), (residue_hbm, residue_flat), (k_hbm, k_ref), (v_hbm, v_ref), (taps_hbm, taps_ref),
             (skip_hbm, skip_ref), (q_hbm, q_ref), (gain_hbm, gain_ref))
    tail_loads = [pltpu.make_async_copy(ref.at[tok - 16:tok, :], tails.at[j], tail_sem.at[j])
                  for j, ref in enumerate((q_hbm, k_hbm, v_hbm))]
    loads = [pltpu.make_async_copy(src, dst, load_sem.at[j]) for j, (src, dst) in enumerate(order)]
    for load in tail_loads + loads:
        load.start()
    barrier = pltpu.get_barrier_semaphore()
    for other in [right, left] + [partner(1 << r) for r in range(rounds)]:
        pl.semaphore_signal(barrier, inc=1, device_id={"seq": other}, device_id_type=MESH)
    for d in range(1, nch):
        pl.semaphore_signal(barrier, inc=1, device_id={"ch": lax.rem(mych + d, nch)}, device_id_type=MESH)

    halo_out[...] = jnp.zeros_like(halo_out)
    for j in range(3):
        tail_loads[j].wait()
        halo_out[2 * j:2 * j + 2, :] = tails[j].astype(f32)[14:16]
    pl.semaphore_wait(barrier, 2 + rounds + nch - 1)

    halo = pltpu.make_async_remote_copy(halo_out, halo_in, halo_send, halo_recv,
                                        device_id={"seq": right}, device_id_type=MESH)

    @pl.when(me < n - 1)
    def _():
        halo.start()

    lane = lax.broadcasted_iota(jnp.int32, (1, LANES), 1)
    lane_group = lane // modes
    lags_rev = (tok - 1 - lax.broadcasted_iota(jnp.int32, (1, tok), 1)).astype(f32)

    spread = (lax.broadcasted_iota(jnp.int32, (modes, LANES), 1) % modes
              == lax.broadcasted_iota(jnp.int32, (modes, LANES), 0)).astype(f32)
    after = (lax.broadcasted_iota(jnp.int32, (tok, 1), 0) + 1).astype(f32)
    sub = lax.broadcasted_iota(jnp.int32, (per, LANES), 0)
    sub_lane = lax.broadcasted_iota(jnp.int32, (per, LANES), 1) // modes

    def prepare(i, _):
        logs = decay_ref[pl.ds(pl.multiple_of(i * per, per), per), :]
        res = residue_ref[pl.ds(pl.multiple_of(i * per, per), per), :]
        pole = jnp.exp(logs)
        weight = res * jnp.sqrt(1.0 - pole * pole)
        cols, wcols = logs.T, weight.T
        rows = []
        wide_rate = jnp.zeros((modes, LANES), f32)
        wide_w = jnp.zeros((modes, LANES), f32)
        for j in range(per):
            col, wcol = cols[:, j:j + 1], wcols[:, j:j + 1]
            power = jnp.exp(col * lags_rev)
            leaving[pl.ds(pl.multiple_of(i * LANES, LANES) + j * modes, modes), :] = power.astype(bf16)
            rows.append(jnp.sum(power * wcol, axis=0, keepdims=True))
            wide_rate = jnp.where(lane_group == j, col, wide_rate)
            wide_w = jnp.where(lane_group == j, wcol, wide_w)
        hrev[pl.ds(pl.multiple_of(i * per, per), per), :] = jnp.concatenate(rows, axis=0)
        rate[:, tile_at(i)] = wide_rate
        wide_weight[:, tile_at(i)] = wide_w
        return 0

    loads[0].wait()
    loads[1].wait()
    decay_ref[...] = decay_flat[...].T
    residue_ref[...] = residue_flat[...].T
    lax.fori_loop(0, tiles, prepare, 0)
    for load in loads[2:6]:
        load.wait()

    @pl.when(me > 0)
    def _():
        halo.wait_recv()

    @pl.when(me == 0)
    def _():
        halo_in[...] = jnp.zeros_like(halo_in)

    def short(ref, which, i, slot=0):
        place = 3 * slot + which
        pad[place, 8:8 + tok, :] = ref[:, tile_at(i)].astype(f32)
        pad[place, 0:8, :] = jnp.concatenate(
            [jnp.zeros((6, LANES), f32), halo_in[2 * which:2 * which + 2, tile_at(i)]], axis=0)
        a = [taps_ref[3 * which + t:3 * which + t + 1, tile_at(i)] for t in range(3)]
        return a[0] * pad[place, 8:8 + tok, :] + a[1] * pad[place, 7:7 + tok, :] + a[2] * pad[place, 6:6 + tok, :]

    def summarize(i, _):
        pair = [2 * i, 2 * i + 1]
        values = [(short(k_ref, 1, t, u) * short(v_ref, 2, t, u)).astype(bf16) for u, t in enumerate(pair)]
        spreadout = [jnp.dot(leaving[tile_at(t), :], values[u], preferred_element_type=f32) for u, t in enumerate(pair)]
        for u, t in enumerate(pair):
            state = jnp.zeros((modes, LANES), f32)
            for j in range(per):
                state = jnp.where(lane_group == j, spreadout[u][j * modes:(j + 1) * modes], state)
            mixed[:, tile_at(t)] = values[u]
            total[:, tile_at(t)] = state
            first_out[:, tile_at(t)] = state.astype(bf16)
        return 0

    lax.fori_loop(0, tiles // 2, summarize, 0)

    causal = (lax.broadcasted_iota(jnp.int32, (half, tok), 1)
              <= lax.broadcasted_iota(jnp.int32, (half, tok), 0) + half)

    def convolve(i, _):
        values = mixed[:, tile_at(i)]
        first, second = values[:half], values[half:]
        right_side = jnp.concatenate(
            [jnp.concatenate([jnp.zeros_like(first), first], axis=1),
             jnp.concatenate([first, second], axis=1)], axis=0)
        lines = hrev[pl.ds(pl.multiple_of(i * per, per), per), :]
        blocks = []
        for j in range(per):
            line = jnp.broadcast_to(lines[j:j + 1], (half, tok))
            block = pltpu.roll(line, half + 1, 1, stride=1, stride_axis=0)
            blocks.append(jnp.where(causal, block, 0.0).astype(bf16))
        product = jnp.dot(jnp.concatenate(blocks, axis=0), right_side, preferred_element_type=f32)
        low = jnp.zeros((half, LANES), f32)
        high = jnp.zeros((half, LANES), f32)
        for j in range(per):
            part = product[j * half:(j + 1) * half]
            low = jnp.where(lane_group == j, part[:, :LANES], low)
            high = jnp.where(lane_group == j, part[:, LANES:], high)
        skip = skip_ref[:, tile_at(i)]
        conv[:half, tile_at(i)] = low + skip * first.astype(f32)
        conv[half:, tile_at(i)] = high + skip * second.astype(f32)
        logs = decay_ref[pl.ds(pl.multiple_of(i * per, per), per), :]
        row = jnp.dot(logs, spread, preferred_element_type=f32, precision=lax.Precision.HIGHEST)
        row = jnp.sum(jnp.where(sub == sub_lane, row, 0.0), axis=0, keepdims=True)
        entering[:, tile_at(i)] = jnp.exp(after * row).astype(bf16)
        q_ref[:, tile_at(i)] = short(q_ref, 0, i).astype(bf16)
        return 0

    loads[6].wait()

    carry[...] = jnp.zeros_like(carry)
    half_tiles = tiles // 2
    core = lax.rem(me, 2)
    lead = max(tiles // 8, 1)
    tail = max(tiles // 16, 1)
    bounds = [0] + [lead + (tiles - lead - tail) * r // (rounds - 1) for r in range(rounds)]
    for r in range(rounds):
        bit = 1 << r
        last = r == rounds - 1
        upper = lax.rem(lax.div(me, bit), 2) == 1
        copy = scan_copy(r)
        if last:
            @pl.when(jnp.logical_not(upper))
            def _():
                copy.start()
        else:
            copy.start()
        lax.fori_loop(bounds[r], bounds[r + 1], convolve, 0)
        block_rate = float(tok * bit)
        offset = ((lax.rem(me, bit) - core) * tok).astype(f32) if r else None

        def merge(i, _):
            place = tile_at(core * half_tiles + i)
            theirs = (state_in[r, :, tile_at(i)] if r else first_in[:, place]).astype(f32)
            logs = rate[:, place]
            if r:
                inward = jnp.exp(logs * offset) * theirs
                carry[:, tile_at(i)] += jnp.where(upper, inward, 0.0)
            if not last:
                mine = total[:, place]
                later = jnp.where(upper, mine, theirs)
                before = jnp.where(upper, theirs, mine)
                both = jnp.exp(logs * block_rate) * before + later
                total[:, place] = both
                state_out[r + 1, :, tile_at(i)] = both.astype(bf16)
            return 0

        if last:
            @pl.when(upper)
            def _():
                copy.wait_recv()
                lax.fori_loop(0, half_tiles, merge, 0)
        else:
            copy.wait_recv()
            lax.fori_loop(0, half_tiles, merge, 0)

    share = pltpu.make_async_remote_copy(carry, carry_in, carry_send, carry_recv,
                                         device_id={"seq": partner(1)}, device_id_type=MESH)
    share.start()
    lax.fori_loop(bounds[rounds], tiles, convolve, 0)
    share.wait()

    def assemble(i, _):
        for part, side in ((carry, core), (carry_in, 1 - core)):
            place = tile_at(side * half_tiles + i)
            entry = part[:, tile_at(i)]
            moved = jnp.exp(rate[:, place] * float(tok)) * entry + first_in[:, place].astype(f32)
            total[:, place] = jnp.where(core == 1, moved, entry)
        return 0

    lax.fori_loop(0, half_tiles, assemble, 0)

    square[...] = jnp.zeros_like(square)
    loads[7].wait()

    def gated_tile(i):
        state = total[:, tile_at(i)] * wide_weight[:, tile_at(i)]
        diagonal = jnp.concatenate([jnp.where(lane_group == j, state, 0.0) for j in range(per)], axis=0)
        fine = diagonal.astype(bf16)
        rest = (diagonal - fine.astype(f32)).astype(bf16)
        ent = entering[:, tile_at(i)]
        carried = jnp.dot(jnp.concatenate([ent, ent], axis=1), jnp.concatenate([fine, rest], axis=0),
                          preferred_element_type=f32)
        return q_ref[:, tile_at(i)].astype(f32) * (conv[:, tile_at(i)] + carried)

    def gate(i, _):
        one, two = gated_tile(2 * i), gated_tile(2 * i + 1)
        conv[:, tile_at(2 * i)] = one
        conv[:, tile_at(2 * i + 1)] = two
        square[...] += one * one + two * two
        return 0

    lax.fori_loop(0, tiles // 2, gate, 0)

    sums = jnp.sum(square[...].T, axis=0, keepdims=True)
    square_out[...] = jnp.broadcast_to(sums, square_out.shape)
    copies = []
    for d in range(1, nch):
        c = pltpu.make_async_remote_copy(square_out, square_in.at[d - 1], square_send.at[d - 1], square_recv.at[d - 1],
                                         device_id={"ch": lax.rem(mych + d, nch)}, device_id_type=MESH)
        c.start()
        copies.append(c)
    for d, c in enumerate(copies):
        c.wait()
        sums = sums + square_in[d, 0:1, :]
    scale = lax.rsqrt(sums / (channels * nch) + 1e-5)
    square[...] = jnp.broadcast_to(scale, (LANES, tok)).T

    def finish(i, _):
        out_ref[:, tile_at(i)] = (conv[:, tile_at(i)] * square[...] * gain_ref[:, tile_at(i)]).astype(bf16)
        return 0

    lax.fori_loop(0, tiles, finish, 0)

    @pl.when(me < n - 1)
    def _():
        halo.wait_send()

    for r in range(rounds):
        bit = 1 << r
        copy = scan_copy(r)
        if r == rounds - 1:
            @pl.when(lax.rem(lax.div(me, bit), 2) == 0)
            def _():
                copy.wait_send()
        else:
            copy.wait_send()


def on_device(n, nch, q_proj, k_proj, v_proj, short_filter, log_decay, residue, skip_bias, norm_gain):
    tok, channels = q_proj.shape
    groups, modes = log_decay.shape
    rounds = n.bit_length() - 1
    assert channels % (2 * LANES) == 0 and n == 1 << rounds and rounds > 1 and channels == groups * modes
    vmem = pl.BlockSpec(memory_space=pltpu.VMEM)
    dma = pltpu.SemaphoreType.DMA
    return pl.pallas_call(
        functools.partial(kernel, n, nch, rounds, modes),
        out_shape=jax.ShapeDtypeStruct((tok, channels), bf16),
        in_specs=[pl.BlockSpec(memory_space=pltpu.HBM)] * 8,
        out_specs=vmem,
        scratch_shapes=[
            pltpu.VMEM((tok, channels), bf16),
            pltpu.VMEM((tok, channels), bf16),
            pltpu.VMEM((tok, channels), bf16),
            pltpu.VMEM((9, channels), f32),
            pltpu.VMEM((modes, groups), f32),
            pltpu.VMEM((modes, groups), f32),
            pltpu.VMEM((1, channels), f32),
            pltpu.VMEM((1, channels), f32),
            pltpu.VMEM((3, 16, channels), bf16),
            pltpu.VMEM((groups, modes), f32),
            pltpu.VMEM((groups, modes), f32),
            pltpu.VMEM((8, channels), f32),
            pltpu.VMEM((8, channels), f32),
            pltpu.VMEM((6, tok + 8, LANES), f32),
            pltpu.VMEM((channels, tok), bf16),
            pltpu.VMEM((groups, tok), f32),
            pltpu.VMEM((tok, channels), bf16),
            pltpu.VMEM((tok, channels), bf16),
            pltpu.VMEM((tok, channels), f32),
            pltpu.VMEM((modes, channels), f32),
            pltpu.VMEM((modes, channels), f32),
            pltpu.VMEM((modes, channels), f32),
            pltpu.VMEM((modes, channels // 2), f32),
            pltpu.VMEM((modes, channels // 2), f32),
            pltpu.VMEM((modes, channels), bf16),
            pltpu.VMEM((modes, channels), bf16),
            pltpu.VMEM((rounds, modes, channels // 2), bf16),
            pltpu.VMEM((rounds, modes, channels // 2), bf16),
            pltpu.VMEM((tok, LANES), f32),
            pltpu.VMEM((8, tok), f32),
            pltpu.VMEM((max(nch - 1, 1), 8, tok), f32),
            dma, dma, dma((rounds,)), dma((rounds,)), dma((max(nch - 1, 1),)), dma((max(nch - 1, 1),)),
            dma((8,)), dma((3,)), dma, dma,
        ],
        compiler_params=pltpu.CompilerParams(collective_id=0, has_side_effects=True,
                                             vmem_limit_bytes=50 * 1024 * 1024),
    )(q_proj, k_proj, v_proj, short_filter, log_decay.T, residue.T,
      skip_bias.reshape(1, channels), norm_gain.reshape(1, channels))


def solution(mesh):
    return jax.shard_map(
        functools.partial(on_device, mesh.shape["seq"], mesh.shape["ch"]),
        mesh=mesh,
        in_specs=(P("seq", "ch"), P("seq", "ch"), P("seq", "ch"), P(None, "ch"),
                  P("ch", None), P("ch", None), P("ch"), P("ch")),
        out_specs=P("seq", "ch"),
        check_vma=False,
    )
```
